256 devices in a mesh: space: 128 (over x, y, z), blk: 2 (over core).
Axes of the slice: x: 4, y: 4, z: 8, core: 2. Of those that a mesh axis runs over, the one named last changes fastest.
Arguments:
- spectra: bfloat16 [4, 2, 64, 1048576], P(None, None, 'blk', 'space'), may hold values from -1600 to 1600
- weights: float32 [1048576], P('space'), may hold values from 0 to 0.00019073486, as said below
- vectors: float32 [4, 2, 64, 8], replicated, may hold values from -0.5 to 0.5
Outputs:
- gram: float32 [4, 2, 64, 64], replicated
- modes: bfloat16 [4, 2, 8, 1048576], P(None, None, None, ('space', 'blk'))
The draws below stay inside these ranges and needn't reach their ends.
Inputs may be any that keep to these rules, and one draw needn't show every extreme that they name: `weights`: positive.
All inputs are finite; a program needn't handle non-finite values.
Results may differ from the reference program's by a relative error of at most 0.0052.
Values may be sent and summed in bfloat16 or wider, within the bound.
A program may use at most 128 MiB of HBM per device.

```python
import math
import jax
import jax.numpy as jnp
from jax import lax

K = 4
M = 64
NMODE = 8
NPTS = 1048576


def draw_spectra(key, part):
    keys = jax.random.split(key, 6)
    noise = jnp.clip(jax.random.normal(keys[0], (K, 2, M, NPTS), jnp.float32), -5.0, 5.0)
    mixing = 0.7
    shared = jnp.clip(jax.random.normal(keys[1], (K, 2, 1, NPTS), jnp.float32), -4.0, 4.0)
    coupling = jnp.clip(jax.random.normal(keys[2], (K, 1, M, 1), jnp.float32), -4.0, 4.0)
    scaling = jnp.exp(jax.random.uniform(keys[3], (K, 1, M, 1), jnp.float32, math.log(0.3), math.log(3.0)))
    active = jax.random.randint(keys[4], (1, 1, 1, NPTS), 0, 256) == 0
    level = jnp.exp(jax.random.uniform(keys[5], (1, 1, 1, NPTS), jnp.float32, math.log(8.0), math.log(64.0)))
    envelope = 0.45 * jnp.where(active, level, 1.0)
    return (scaling * envelope * (noise + mixing * coupling * shared)).astype(jnp.bfloat16)


def draw_weights(key, part):
    position = jnp.arange(NPTS, dtype=jnp.float32) / NPTS
    spread = jnp.exp(jax.random.uniform(key, (NPTS,), jnp.float32, math.log(0.3), math.log(3.0)))
    ramp = 0.5 + position
    return 32.0 / NPTS * spread * ramp


def scatter_about(own_key, extent, scale, reach, held_as=jnp.bfloat16):
    return jnp.clip(scale * jax.random.normal(own_key, extent, jnp.float32), -reach, reach).astype(held_as)


def setup_inputs(seed: int = 0) -> dict:
    key_of = jax.random.split(jax.random.key(seed), 4)
    return {
        "spectra": draw_spectra(jax.random.fold_in(key_of[3], 71), 0),
        "weights": draw_weights(jax.random.fold_in(key_of[3], 71), 0),
        "vectors": scatter_about(key_of[2], (K, 2, M, NMODE), (2 * M) ** -0.5, 0.5, jnp.float32),
    }


def reference(spectra, weights, vectors):
    hp = lax.Precision.HIGHEST
    grams = []
    modes = []
    for k in range(K):
        stacked = spectra[k].reshape(2 * M, NPTS)
        weighted = (stacked.astype(jnp.float32) * weights[None, :]).astype(jnp.bfloat16)
        products = lax.dot_general(weighted, stacked, (((1,), (1,)), ((), ())), preferred_element_type=jnp.float32)
        real_part = (products[:M, :M] + products[M:, M:]) / M
        imag_part = (products[:M, M:] - products[M:, :M]) / M
        grams.append(jnp.stack([real_part, imag_part]))
        vec_re = vectors[k, 0]
        vec_im = vectors[k, 1]
        prod_re = jnp.dot(real_part, vec_re, precision=hp) - jnp.dot(imag_part, vec_im, precision=hp)
        prod_im = jnp.dot(real_part, vec_im, precision=hp) + jnp.dot(imag_part, vec_re, precision=hp)
        lam = lax.optimization_barrier(jnp.sum(vec_re * prod_re + vec_im * prod_im, axis=0))
        psi_b = vectors[k].astype(jnp.bfloat16)
        upper = jnp.concatenate([psi_b[0], -psi_b[1]], axis=0)
        lower = jnp.concatenate([psi_b[1], psi_b[0]], axis=0)
        raw_re = lax.dot_general(upper, stacked, (((0,), (0,)), ((), ())), preferred_element_type=jnp.float32)
        raw_im = lax.dot_general(lower, stacked, (((0,), (0,)), ((), ())), preferred_element_type=jnp.float32)
        factor = lax.rsqrt(lam + 1e-06)[:, None]
        modes.append(jnp.stack([raw_re * factor, raw_im * factor]).astype(jnp.bfloat16))
    return (jnp.stack(grams), jnp.stack(modes))
```

```python
import jax
import jax.numpy as jnp
from jax import lax
from jax.experimental import pallas as pl
from jax.experimental.pallas import tpu as pltpu
from jax.sharding import PartitionSpec as P

MESH = pl.DeviceIdType.MESH
K, M, N = 4, 64, 8
NX, NY, NZ = 4, 4, 8
PLANE = NX * NY
BINS = K // 2
HALF = M // 2
ROWS = 48
CHUNKS = 2
TILE = 1024
XY, Z = 0, 1


def ring_distance(d, n):
    return min(d, n - d)


STEPS_XY = sorted(
    ((dx, dy) for dx in range(NX) for dy in range(NY) if dx or dy),
    key=lambda d: -ring_distance(d[0], NX) - ring_distance(d[1], NY),
)
STEPS_Z = sorted(range(1, NZ), key=lambda d: -ring_distance(d, NZ))


def kernel(
    spec, wts, vec, gram, modes,
    s_all, w, v, mix, raw, box_xy, box_z, gram_out, modes_out,
    pair, all_in, load_sem, small_sem, swap_send, swap_recv, sum_send, sum_recv, out_sem, out_send, out_recv,
):
    here = lax.axis_index("space")
    core = lax.axis_index("blk")
    x, y, z = here // (NY * NZ), (here // NZ) % NY, here % NZ
    points = s_all.shape[3]
    span = points // CHUNKS
    share = points // 2
    sibling = (here, 1 - core)
    first = core * BINS
    peers = {
        XY: [((((x + dx) % NX) * NY + (y + dy) % NY) * NZ + z, core) for dx, dy in STEPS_XY],
        Z: [((x * NY + y) * NZ + (z + d) % NZ, core) for d in STEPS_Z],
    }
    boxes = {XY: box_xy, Z: box_z}
    slots = {XY: x * NY + y, Z: z}

    w_copy = pltpu.make_async_copy(wts, w, small_sem.at[0])
    v_copy = pltpu.make_async_copy(vec.at[pl.ds(first, BINS)], v, small_sem.at[1])
    v_copy.start()
    w_copy.start()
    rows = pl.ds(pl.multiple_of(core * HALF, HALF), HALF)
    loads, swaps = {}, {}
    for k in range(BINS):
        for h in range(CHUNKS):
            cols = pl.ds(h * span, span)
            loads[k, h] = pltpu.make_async_copy(
                spec.at[first + k, :, :, cols], s_all.at[k, :, rows, cols], load_sem.at[k, h]
            )
            swaps[k, h] = pltpu.make_async_remote_copy(
                src_ref=spec.at[BINS - first + k, :, :, cols],
                dst_ref=s_all.at[k, :, rows, cols],
                send_sem=swap_send.at[k, h],
                recv_sem=swap_recv.at[k, h],
                device_id=sibling,
                device_id_type=MESH,
            )

    barrier = pltpu.get_barrier_semaphore()

    @pl.when(core == 1)
    def _():
        pl.semaphore_signal(barrier, inc=1, device_id=(here, 0), device_id_type=MESH)

    @pl.when(core == 0)
    def _():
        pl.semaphore_wait(barrier, 1)
        pl.semaphore_signal(pair, inc=1, device_id=(here, 1), device_id_type=MESH)

    @pl.when(core == 1)
    def _():
        pl.semaphore_wait(pair, 1)

    for k in range(BINS):
        for h in range(CHUNKS):
            swaps[k, h].start()
            loads[k, h].start()

    @pl.when(core == 1)
    def _():
        for t, _ in peers[XY] + peers[Z]:
            pl.semaphore_signal(barrier, inc=1, device_id=(t, 1), device_id_type=MESH)

    v_copy.wait()
    for k in range(BINS):
        re, im = v[k, 0], v[k, 1]
        both = jnp.concatenate(
            [jnp.concatenate([re, -im], axis=1), jnp.concatenate([im, re], axis=1)], axis=0
        )
        high = both.astype(jnp.bfloat16).astype(jnp.float32)
        mix[k] = jnp.concatenate([high, both - high], axis=0).astype(jnp.bfloat16)
    w_copy.wait()

    def products(k):
        total = jnp.zeros((2 * M, 2 * M), jnp.float32)
        power = jnp.zeros((N, 128), jnp.float32)
        mixer = mix[k]
        for h in range(CHUNKS):
            loads[k, h].wait()
            swaps[k, h].wait_recv()

            def step(i, carry):
                total, power = carry
                cols = pl.ds(pl.multiple_of(h * span + i * TILE, TILE), TILE)
                s = s_all[k, :, :, cols].reshape(2 * M, TILE)
                wt = w[:, cols]
                weighted = (s.astype(jnp.float32) * wt).astype(jnp.bfloat16)
                total += lax.dot_general(
                    weighted, s, (((1,), (1,)), ((), ())), preferred_element_type=jnp.float32
                )
                r = jnp.dot(mixer, s, preferred_element_type=jnp.float32)
                raw[k, :, cols] = r[: 2 * N]
                full = r[: 2 * N] + r[2 * N :]
                square = full * full
                square = (square[:N] + square[N:]) * wt
                for g in range(TILE // 128):
                    power += square[:, g * 128 : (g + 1) * 128]
                return total, power

            total, power = lax.fori_loop(0, span // TILE, step, (total, power))
        return total, power

    row = lax.broadcasted_iota(jnp.int32, (M, 128), 0)
    lane = lax.broadcasted_iota(jnp.int32, (M, 128), 1)

    def message(packed, power):
        high = power.astype(jnp.bfloat16).astype(jnp.float32)
        return jnp.concatenate([packed, high, power - high], axis=0).astype(jnp.bfloat16)

    def pack(total):
        turned = pltpu.roll(total, M, 1)
        real = total[:M] + turned[M:]
        imag = turned[:M] - total[M:]
        held = jnp.where(row >= lane, real, imag)
        return jnp.where(lane[:HALF] < M, held[:HALF], pltpu.roll(held, M, 1)[HALF:])

    def send(k, axis, what):
        box = boxes[axis].at[k, slots[axis]]
        box[...] = what
        for t in peers[axis]:
            pltpu.make_async_remote_copy(
                src_ref=box,
                dst_ref=box,
                send_sem=sum_send.at[k, axis],
                recv_sem=sum_recv.at[k, axis],
                device_id=t,
                device_id_type=MESH,
            ).start()

    def all_others(k, axis):
        return boxes[axis].at[k, pl.ds(0, len(peers[axis]))]

    def gather(k, axis):
        ref = all_others(k, axis)
        pltpu.make_async_copy(ref, ref, sum_recv.at[k, axis]).wait()
        got = boxes[axis][k].astype(jnp.float32)
        got = jnp.sum(got, axis=0)
        return got[:HALF], got[HALF : HALF + N] + got[HALF + N :]

    outs = []

    def finish(k, packed, power):
        lam = jnp.sum(power, axis=1, keepdims=True) / M
        factor = lax.rsqrt(lam + 1e-06)
        factor = jnp.concatenate([factor, factor], axis=0)
        modes_out[k] = (raw[k] * factor).astype(jnp.bfloat16)
        own = modes_out.at[k, :, pl.ds(pl.multiple_of(core * share, share), share)]
        other = modes_out.at[k, :, pl.ds(pl.multiple_of((1 - core) * share, share), share)]
        put(2 * k, own, other, modes.at[first + k])
        packed = packed / M
        held = jnp.concatenate([packed, pltpu.roll(packed, M, 1)], axis=0)
        across = jnp.concatenate([held, held], axis=0).T[:M]
        real = jnp.where(row >= lane, held, across)
        imag = jnp.where(row < lane, held, jnp.where(row > lane, -across, 0.0))
        gram_out[k, 0] = real[:, :M]
        gram_out[k, 1] = imag[:, :M]
        put(2 * k + 1, gram_out.at[k], gram_out.at[k], gram.at[first + k])

    def put(i, own, other, target):
        away = pltpu.make_async_remote_copy(
            src_ref=other,
            dst_ref=target,
            send_sem=out_send.at[i],
            recv_sem=out_recv.at[i],
            device_id=sibling,
            device_id_type=MESH,
        )
        home = pltpu.make_async_copy(own, target, out_sem.at[i])
        away.start()
        home.start()
        outs.append((away, home))

    total, power = products(0)

    @pl.when(core == 1)
    def _():
        pl.semaphore_wait(barrier, len(STEPS_XY) + len(STEPS_Z))
        pl.semaphore_signal(all_in, inc=1, device_id=(here, 0), device_id_type=MESH)

    @pl.when(core == 0)
    def _():
        pl.semaphore_wait(all_in, 1)

    send(0, XY, message(pack(total), power))
    total, power = products(1)
    send(1, Z, message(pack(total), power))
    send(0, Z, message(*gather(0, XY)))
    send(1, XY, message(*gather(1, Z)))
    finish(0, *gather(0, Z))
    finish(1, *gather(1, XY))

    for k in range(BINS):
        for h in range(CHUNKS):
            swaps[k, h].wait_send()
        for axis in (XY, Z):
            ref = all_others(k, axis)
            pltpu.make_async_copy(ref, ref, sum_send.at[k, axis]).wait()
    for away, home in outs:
        away.wait()
        home.wait()


def on_device(spectra, weights, vectors):
    points = spectra.shape[3]
    dma = pltpu.SemaphoreType.DMA
    gram, modes = pl.pallas_call(
        kernel,
        out_shape=(
            jax.ShapeDtypeStruct((K, 2, M, M), jnp.float32),
            jax.ShapeDtypeStruct((K, 2 * N, points // 2), jnp.bfloat16),
        ),
        in_specs=[pl.BlockSpec(memory_space=pl.ANY)] * 3,
        out_specs=[pl.BlockSpec(memory_space=pl.ANY)] * 2,
        scratch_shapes=[
            pltpu.VMEM((BINS, 2, M, points), jnp.bfloat16),
            pltpu.VMEM((1, points), jnp.float32),
            pltpu.VMEM((BINS, 2, N, M), jnp.float32),
            pltpu.VMEM((BINS, 4 * N, 2 * M), jnp.bfloat16),
            pltpu.VMEM((BINS, 2 * N, points), jnp.float32),
            pltpu.VMEM((BINS, PLANE, ROWS, 128), jnp.bfloat16),
            pltpu.VMEM((BINS, NZ, ROWS, 128), jnp.bfloat16),
            pltpu.VMEM((BINS, 2, M, M), jnp.float32),
            pltpu.VMEM((BINS, 2 * N, points), jnp.bfloat16),
            pltpu.SemaphoreType.REGULAR,
            pltpu.SemaphoreType.REGULAR,
            dma((BINS, CHUNKS)),
            dma((2,)),
            dma((BINS, CHUNKS)),
            dma((BINS, CHUNKS)),
            dma((BINS, 2)),
            dma((BINS, 2)),
            dma((2 * BINS,)),
            dma((2 * BINS,)),
            dma((2 * BINS,)),
        ],
        compiler_params=pltpu.CompilerParams(
            collective_id=0, has_side_effects=True, vmem_limit_bytes=56 * 1024 * 1024
        ),
    )(spectra, weights.reshape(1, points), jnp.swapaxes(vectors, 2, 3))
    return gram, modes.reshape(K, 2, N, points // 2)


def solution(mesh):
    return jax.shard_map(
        on_device,
        mesh=mesh,
        in_specs=(P(None, None, "blk", "space"), P("space"), P()),
        out_specs=(P(), P(None, None, None, ("space", "blk"))),
        check_vma=False,
    )
```

```python
import jax
import jax.numpy as jnp
from jax import lax
from jax.experimental import pallas as pl
from jax.experimental.pallas import tpu as pltpu
from jax.sharding import PartitionSpec as P

MESH = pl.DeviceIdType.MESH
K, M, N = 4, 64, 8
NX, NY, NZ = 4, 4, 8
PLANE = NX * NY
BINS = K // 2
HALF = M // 2
ROWS = 48
XY, Z = 0, 1


def ring_distance(d, n):
    return min(d, n - d)


STEPS_XY = sorted(
    ((dx, dy) for dx in range(NX) for dy in range(NY) if dx or dy),
    key=lambda d: -ring_distance(d[0], NX) - ring_distance(d[1], NY),
)
STEPS_Z = sorted(range(1, NZ), key=lambda d: -ring_distance(d, NZ))


def positions():
    return [lax.broadcasted_iota(jnp.int32, (M, 128), d) for d in (0, 1)]


def kernel(
    spec, wts, vec, raw, sums,
    s_all, w, v, mix, raw_away, box_xy, box_z,
    pair, all_in, load_sem, small_sem, swap_send, swap_recv, sum_send, sum_recv, out_send, out_recv,
):
    here = lax.axis_index("space")
    core = lax.axis_index("blk")
    x, y, z = here // (NY * NZ), (here // NZ) % NY, here % NZ
    points = s_all.shape[3]
    share = points // 2
    sibling = (here, 1 - core)
    first = core * BINS
    peers = {
        XY: [((((x + dx) % NX) * NY + (y + dy) % NY) * NZ + z, core) for dx, dy in STEPS_XY],
        Z: [((x * NY + y) * NZ + (z + d) % NZ, core) for d in STEPS_Z],
    }
    boxes = {XY: box_xy, Z: box_z}
    slots = {XY: x * NY + y, Z: z}

    w_copy = pltpu.make_async_copy(wts, w, small_sem.at[0])
    v_copy = pltpu.make_async_copy(vec.at[pl.ds(first, BINS)], v, small_sem.at[1])
    v_copy.start()
    w_copy.start()
    rows = pl.ds(pl.multiple_of(core * HALF, HALF), HALF)
    halves = [
        pl.ds(pl.multiple_of((1 - core) * share, share), share),
        pl.ds(pl.multiple_of(core * share, share), share),
    ]
    loads, swaps = {}, {}
    for k in range(BINS):
        for h, theirs in ((0, 1), (1, 0)):
            cols = halves[h]
            loads[k, h] = pltpu.make_async_copy(
                spec.at[first + k, :, :, cols], s_all.at[k, :, rows, cols], load_sem.at[k, h]
            )
            cols = halves[theirs]
            swaps[k, h] = pltpu.make_async_remote_copy(
                src_ref=spec.at[BINS - first + k, :, :, cols],
                dst_ref=s_all.at[k, :, rows, cols],
                send_sem=swap_send.at[k, h],
                recv_sem=swap_recv.at[k, h],
                device_id=sibling,
                device_id_type=MESH,
            )

    barrier = pltpu.get_barrier_semaphore()

    @pl.when(core == 1)
    def _():
        pl.semaphore_signal(barrier, inc=1, device_id=(here, 0), device_id_type=MESH)

    @pl.when(core == 0)
    def _():
        pl.semaphore_wait(barrier, 1)
        pl.semaphore_signal(pair, inc=1, device_id=(here, 1), device_id_type=MESH)

    @pl.when(core == 1)
    def _():
        pl.semaphore_wait(pair, 1)

    for k in range(BINS):
        for h in range(2):
            swaps[k, h].start()
            loads[k, h].start()

    @pl.when(core == 1)
    def _():
        for t, _ in peers[XY] + peers[Z]:
            pl.semaphore_signal(barrier, inc=1, device_id=(t, 1), device_id_type=MESH)

    v_copy.wait()
    for k in range(BINS):
        re, im = v[k, 0], v[k, 1]
        both = jnp.concatenate(
            [jnp.concatenate([re, -im], axis=1), jnp.concatenate([im, re], axis=1)], axis=0
        )
        high = both.astype(jnp.bfloat16).astype(jnp.float32)
        mix[k] = jnp.concatenate([high, both - high], axis=0).astype(jnp.bfloat16)
    w_copy.wait()

    def products(k):
        total = jnp.zeros((2 * M, 2 * M), jnp.float32)
        power = jnp.zeros((N, 128), jnp.float32)
        mixer = mix[k]
        for h in range(2):
            loads[k, h].wait()
            swaps[k, h].wait_recv()

            s = s_all[k, :, :, halves[h]].reshape(2 * M, share)
            wt = w[:, halves[h]]
            weighted = (s.astype(jnp.float32) * wt).astype(jnp.bfloat16)
            total += lax.dot_general(
                weighted, s, (((1,), (1,)), ((), ())), preferred_element_type=jnp.float32
            )
            r = jnp.dot(mixer, s, preferred_element_type=jnp.float32)
            if h == 0:
                raw_away[k] = r[: 2 * N]
            else:
                raw[first + k] = r[: 2 * N]
            full = r[: 2 * N] + r[2 * N :]
            square = full * full
            square = (square[:N] + square[N:]) * wt
            for g in range(share // 128):
                power += square[:, g * 128 : (g + 1) * 128]
        return total, power

    row, lane = positions()

    def message(packed, power):
        high = power.astype(jnp.bfloat16).astype(jnp.float32)
        return jnp.concatenate([packed, high, power - high], axis=0).astype(jnp.bfloat16)

    def pack(total):
        turned = pltpu.roll(total, M, 1)
        real = total[:M] + turned[M:]
        imag = turned[:M] - total[M:]
        held = jnp.where(row >= lane, real, imag)
        return jnp.where(lane[:HALF] < M, held[:HALF], pltpu.roll(held, M, 1)[HALF:])

    def send(k, axis, what):
        box = boxes[axis].at[k, slots[axis]]
        box[...] = what
        for t in peers[axis]:
            pltpu.make_async_remote_copy(
                src_ref=box,
                dst_ref=box,
                send_sem=sum_send.at[k, axis],
                recv_sem=sum_recv.at[k, axis],
                device_id=t,
                device_id_type=MESH,
            ).start()

    def all_others(k, axis):
        return boxes[axis].at[k, pl.ds(0, len(peers[axis]))]

    def gather(k, axis):
        ref = all_others(k, axis)
        pltpu.make_async_copy(ref, ref, sum_recv.at[k, axis]).wait()
        got = boxes[axis][k].astype(jnp.float32)
        got = jnp.sum(got, axis=0)
        return got[:HALF], got[HALF : HALF + N] + got[HALF + N :]

    def to_sibling(i, ours, target):
        return pltpu.make_async_remote_copy(
            src_ref=ours,
            dst_ref=target,
            send_sem=out_send.at[i],
            recv_sem=out_recv.at[i],
            device_id=sibling,
            device_id_type=MESH,
        )

    outs = []

    def finish(k, packed, power):
        sums[first + k] = jnp.concatenate([packed, power], axis=0)
        outs.append(to_sibling(BINS + k, sums.at[first + k], sums.at[first + k]))
        outs[-1].start()

    total, power = products(0)

    @pl.when(core == 1)
    def _():
        pl.semaphore_wait(barrier, len(STEPS_XY) + len(STEPS_Z))
        pl.semaphore_signal(all_in, inc=1, device_id=(here, 0), device_id_type=MESH)

    @pl.when(core == 0)
    def _():
        pl.semaphore_wait(all_in, 1)

    send(0, XY, message(pack(total), power))
    total, power = products(1)
    send(1, Z, message(pack(total), power))
    for k in range(BINS):
        outs.append(to_sibling(k, raw_away.at[k], raw.at[first + k]))
        outs[-1].start()
    send(0, Z, message(*gather(0, XY)))
    send(1, XY, message(*gather(1, Z)))
    finish(0, *gather(0, Z))
    finish(1, *gather(1, XY))

    for k in range(BINS):
        for h in range(2):
            swaps[k, h].wait_send()
        for axis in (XY, Z):
            ref = all_others(k, axis)
            pltpu.make_async_copy(ref, ref, sum_send.at[k, axis]).wait()
    for copy in outs:
        copy.wait()


def finish_kernel(raw, sums, gram, modes, gram_out, modes_out, sem):
    row, lane = positions()
    copies = []

    def write(i, source, target):
        copies.append(pltpu.make_async_copy(source, target, sem.at[i]))
        copies[-1].start()

    for k in range(K):
        lam = jnp.sum(sums[k, HALF:], axis=1, keepdims=True) / M
        factor = lax.rsqrt(lam + 1e-06)
        factor = jnp.concatenate([factor, factor], axis=0)
        modes_out[k] = (raw[k] * factor).astype(jnp.bfloat16)
        write(k, modes_out.at[k], modes.at[k])
    for k in range(K):
        packed = sums[k, :HALF] / M
        held = jnp.concatenate([packed, pltpu.roll(packed, M, 1)], axis=0)
        across = jnp.concatenate([held, held], axis=0).T[:M]
        real = jnp.where(row >= lane, held, across)
        imag = jnp.where(row < lane, held, jnp.where(row > lane, -across, 0.0))
        gram_out[k, 0] = real[:, :M]
        gram_out[k, 1] = imag[:, :M]
        write(K + k, gram_out.at[k], gram.at[k])
    for copy in copies:
        copy.wait()


def on_device(spectra, weights, vectors):
    points = spectra.shape[3]
    share = points // 2
    dma = pltpu.SemaphoreType.DMA
    vmem = pl.BlockSpec(memory_space=pltpu.VMEM)
    anywhere = pl.BlockSpec(memory_space=pl.ANY)
    raw, sums = pl.pallas_call(
        kernel,
        out_shape=(
            pltpu.VMEM((K, 2 * N, share), jnp.float32),
            pltpu.VMEM((K, HALF + N, 128), jnp.float32),
        ),
        in_specs=[anywhere] * 3,
        out_specs=[vmem] * 2,
        scratch_shapes=[
            pltpu.VMEM((BINS, 2, M, points), jnp.bfloat16),
            pltpu.VMEM((1, points), jnp.float32),
            pltpu.VMEM((BINS, 2, N, M), jnp.float32),
            pltpu.VMEM((BINS, 4 * N, 2 * M), jnp.bfloat16),
            pltpu.VMEM((BINS, 2 * N, share), jnp.float32),
            pltpu.VMEM((BINS, PLANE, ROWS, 128), jnp.bfloat16),
            pltpu.VMEM((BINS, NZ, ROWS, 128), jnp.bfloat16),
            pltpu.SemaphoreType.REGULAR,
            pltpu.SemaphoreType.REGULAR,
            dma((BINS, 2)),
            dma((2,)),
            dma((BINS, 2)),
            dma((BINS, 2)),
            dma((BINS, 2)),
            dma((BINS, 2)),
            dma((2 * BINS,)),
            dma((2 * BINS,)),
        ],
        compiler_params=pltpu.CompilerParams(
            collective_id=0, has_side_effects=True, vmem_limit_bytes=32 * 1024 * 1024
        ),
    )(
        pltpu.with_memory_space_constraint(spectra, pltpu.HBM),
        pltpu.with_memory_space_constraint(weights.reshape(1, points), pltpu.HBM),
        pltpu.with_memory_space_constraint(jnp.swapaxes(vectors, 2, 3), pltpu.HBM),
    )
    gram, modes = pl.pallas_call(
        finish_kernel,
        out_shape=(
            jax.ShapeDtypeStruct((K, 2, M, M), jnp.float32),
            jax.ShapeDtypeStruct((K, 2 * N, share), jnp.bfloat16),
        ),
        in_specs=[vmem] * 2,
        out_specs=[anywhere] * 2,
        scratch_shapes=[
            pltpu.VMEM((K, 2, M, M), jnp.float32),
            pltpu.VMEM((K, 2 * N, share), jnp.bfloat16),
            dma((2 * K,)),
        ],
    )(
        pltpu.with_memory_space_constraint(raw, pltpu.VMEM),
        pltpu.with_memory_space_constraint(sums, pltpu.VMEM),
    )
    return gram, modes.reshape(K, 2, N, share)


def solution(mesh):
    return jax.shard_map(
        on_device,
        mesh=mesh,
        in_specs=(P(None, None, "blk", "space"), P("space"), P()),
        out_specs=(P(), P(None, None, None, ("space", "blk"))),
        check_vma=False,
    )
```

```python
import jax
import jax.numpy as jnp
from jax import lax
from jax.experimental import pallas as pl
from jax.experimental.pallas import tpu as pltpu
from jax.sharding import PartitionSpec as P

MESH = pl.DeviceIdType.MESH
K, M, N = 4, 64, 8
NX, NY, NZ = 4, 4, 8
PLANE = NX * NY
BINS = K // 2
HALF = M // 2
ROWS = 48
SPLIT = 1
PARTS = 2 * SPLIT
XY, Z = 0, 1


def ring_distance(d, n):
    return min(d, n - d)


STEPS_XY = sorted(
    ((dx, dy) for dx in range(NX) for dy in range(NY) if dx or dy),
    key=lambda d: -ring_distance(d[0], NX) - ring_distance(d[1], NY),
)
STEPS_Z = sorted(range(1, NZ), key=lambda d: -ring_distance(d, NZ))


def positions():
    return [lax.broadcasted_iota(jnp.int32, (M, 128), d) for d in (0, 1)]


def kernel(
    spec, wts, vec, raw, sums,
    s_all, w, v, mix, raw_both, total, power, box_xy, box_z, box_other,
    pair, all_in, load_sem, small_sem, swap_send, swap_recv, sum_send, sum_recv, other_sem, keep_sem, out_send, out_recv,
):
    here = lax.axis_index("space")
    core = lax.axis_index("blk")
    x, y, z = here // (NY * NZ), (here // NZ) % NY, here % NZ
    points = s_all.shape[3]
    share = points // 2
    sibling = (here, 1 - core)
    first = core * BINS
    boxes = {XY: box_xy, Z: box_z}
    slots = {XY: x * NY + y, Z: z}

    barrier = pltpu.get_barrier_semaphore()

    @pl.when(core == 1)
    def _():
        pl.semaphore_signal(barrier, inc=1, device_id=(here, 0), device_id_type=MESH)

    @pl.when(core == 0)
    def _():
        pl.semaphore_wait(barrier, 1)
        pl.semaphore_signal(pair, inc=1, device_id=(here, 1), device_id_type=MESH)

    @pl.when(core == 1)
    def _():
        pl.semaphore_wait(pair, 1)

    w_copy = pltpu.make_async_copy(wts, w, small_sem.at[0])
    v_copy = pltpu.make_async_copy(vec.at[pl.ds(first, BINS)], v, small_sem.at[1])
    v_copy.start()
    w_copy.start()
    rows = pl.ds(pl.multiple_of(core * HALF, HALF), HALF)
    span = share // SPLIT

    def columns(half, part):
        return pl.ds(pl.multiple_of(half * share + part * span, span), span)

    def load(k, part):
        cols = columns(lax.rem(1 - core + part // SPLIT, 2), part % SPLIT)
        return pltpu.make_async_copy(
            spec.at[first + k, :, :, cols], s_all.at[k, :, rows, cols], load_sem.at[k, part]
        )

    def swap(k, part):
        cols = columns(lax.rem(core + part // SPLIT, 2), part % SPLIT)
        return pltpu.make_async_remote_copy(
            src_ref=spec.at[BINS - first + k, :, :, cols],
            dst_ref=s_all.at[k, :, rows, cols],
            send_sem=swap_send.at[k, part],
            recv_sem=swap_recv.at[k, part],
            device_id=sibling,
            device_id_type=MESH,
        )

    for k in range(BINS):
        for part in range(PARTS):
            swap(k, part).start()
            load(k, part).start()

    peers = {
        XY: [((((x + dx) % NX) * NY + (y + dy) % NY) * NZ + z, core) for dx, dy in STEPS_XY],
        Z: [((x * NY + y) * NZ + (z + d) % NZ, core) for d in STEPS_Z],
    }

    @pl.when(core == 1)
    def _():
        for t, _ in peers[XY] + peers[Z]:
            pl.semaphore_signal(barrier, inc=1, device_id=(t, 1), device_id_type=MESH)

    v_copy.wait()
    for k in range(BINS):
        re, im = v[k, 0], v[k, 1]
        both = jnp.concatenate(
            [jnp.concatenate([re, -im], axis=1), jnp.concatenate([im, re], axis=1)], axis=0
        )
        high = both.astype(jnp.bfloat16).astype(jnp.float32)
        mix[k] = jnp.concatenate([high, both - high], axis=0).astype(jnp.bfloat16)
    w_copy.wait()

    row, lane = positions()

    def message(packed, power):
        high = power.astype(jnp.bfloat16).astype(jnp.float32)
        return jnp.concatenate([packed, high, power - high], axis=0).astype(jnp.bfloat16)

    def pack(total):
        turned = pltpu.roll(total, M, 1)
        real = total[:M] + turned[M:]
        imag = turned[:M] - total[M:]
        held = jnp.where(row >= lane, real, imag)
        return jnp.where(lane[:HALF] < M, held[:HALF], pltpu.roll(held, M, 1)[HALF:])

    def send(k, axis, what, both=False):
        box = boxes[axis].at[k, slots[axis]]
        box[...] = what

        def other(t):
            pltpu.make_async_remote_copy(
                src_ref=box,
                dst_ref=box_other.at[slots[axis]],
                send_sem=other_sem.at[0],
                recv_sem=other_sem.at[1],
                device_id=(t, 1 - core),
                device_id_type=MESH,
            ).start()

        for t in peers[axis]:
            pltpu.make_async_remote_copy(
                src_ref=box,
                dst_ref=box,
                send_sem=sum_send.at[k, axis],
                recv_sem=sum_recv.at[k, axis],
                device_id=t,
                device_id_type=MESH,
            ).start()
            if both:
                other(t[0])
        if both:
            other(here)

    def all_others(k, axis):
        return boxes[axis].at[k, pl.ds(0, len(peers[axis]))]

    def gather(k, axis):
        ref = all_others(k, axis)
        pltpu.make_async_copy(ref, ref, sum_recv.at[k, axis]).wait()
        return add_up(boxes[axis][k])

    def add_up(got):
        got = jnp.sum(got.astype(jnp.float32), axis=0)
        return got[:HALF], got[HALF : HALF + N] + got[HALF + N :]

    def to_sibling(i, ours, target):
        return pltpu.make_async_remote_copy(
            src_ref=ours,
            dst_ref=target,
            send_sem=out_send.at[i],
            recv_sem=out_recv.at[i],
            device_id=sibling,
            device_id_type=MESH,
        )

    outs = []

    def finish(at, packed, power):
        sums[at] = jnp.concatenate([packed, power], axis=0)

    total[...] = jnp.zeros_like(total)
    power[...] = jnp.zeros_like(power)

    @pl.loop(0, BINS * PARTS)
    def _(i):
        k, part = i // PARTS, i % PARTS
        cols = columns(lax.rem(1 - core + part // SPLIT, 2), part % SPLIT)
        load(k, part).wait()
        swap(k, part).wait_recv()
        s = s_all[k, :, :, cols].reshape(2 * M, span)
        wt = w[:, cols]
        weighted = (s.astype(jnp.float32) * wt).astype(jnp.bfloat16)
        total[k] += lax.dot_general(
            weighted, s, (((1,), (1,)), ((), ())), preferred_element_type=jnp.float32
        )
        r = jnp.dot(mix[k], s, preferred_element_type=jnp.float32)
        raw_both[k, part // SPLIT, :, pl.ds(pl.multiple_of(part % SPLIT * span, span), span)] = r[: 2 * N]
        full = r[: 2 * N] + r[2 * N :]
        square = full * full
        square = (square[:N] + square[N:]) * wt
        power[k] += sum(square[:, g : g + 128] for g in range(0, span, 128))

        @pl.when(i == PARTS - 1)
        def _():
            @pl.when(core == 1)
            def _():
                pl.semaphore_wait(barrier, len(STEPS_XY) + len(STEPS_Z))
                pl.semaphore_signal(all_in, inc=1, device_id=(here, 0), device_id_type=MESH)

            @pl.when(core == 0)
            def _():
                pl.semaphore_wait(all_in, 1)

            send(0, XY, message(pack(total[0]), power[0]))

    send(1, Z, message(pack(total[1]), power[1]))
    for k in range(BINS):
        keep = pltpu.make_async_copy(raw_both.at[k, 1], raw.at[first + k], keep_sem.at[k])
        keep.start()
        outs.append(keep)
        outs.append(to_sibling(k, raw_both.at[k, 0], raw.at[first + k]))
        outs[-1].start()
    send(0, Z, message(*gather(0, XY)))
    send(1, XY, message(*gather(1, Z)), both=True)
    finish(first, *gather(0, Z))
    outs.append(to_sibling(BINS, sums.at[first], sums.at[first]))
    outs[-1].start()
    finish(first + 1, *gather(1, XY))
    pltpu.make_async_copy(box_other, box_other, other_sem.at[1]).wait()
    finish(BINS - first + 1, *add_up(box_other[...]))

    for k in range(BINS):
        for part in range(PARTS):
            swap(k, part).wait_send()
        for axis in (XY, Z):
            ref = all_others(k, axis)
            pltpu.make_async_copy(ref, ref, sum_send.at[k, axis]).wait()
    pltpu.make_async_copy(box_other, box_other, other_sem.at[0]).wait()
    for copy in outs:
        copy.wait()


def finish_kernel(raw, sums, gram, modes, gram_out, modes_out, sem):
    row, lane = positions()
    copies = []

    def write(i, source, target):
        copies.append(pltpu.make_async_copy(source, target, sem.at[i]))
        copies[-1].start()

    for k in range(K):
        lam = jnp.sum(sums[k, HALF:], axis=1, keepdims=True) / M
        factor = lax.rsqrt(lam + 1e-06)
        factor = jnp.concatenate([factor, factor], axis=0)
        modes_out[k] = (raw[k] * factor).astype(jnp.bfloat16)
        write(k, modes_out.at[k], modes.at[k])
    for k in range(K):
        packed = sums[k, :HALF] / M
        held = jnp.concatenate([packed, pltpu.roll(packed, M, 1)], axis=0)
        across = jnp.concatenate([held, held], axis=0).T[:M]
        real = jnp.where(row >= lane, held, across)
        imag = jnp.where(row < lane, held, jnp.where(row > lane, -across, 0.0))
        gram_out[k, 0] = real[:, :M]
        gram_out[k, 1] = imag[:, :M]
        write(K + k, gram_out.at[k], gram.at[k])
    for copy in copies:
        copy.wait()


def on_device(spectra, weights, vectors):
    points = spectra.shape[3]
    share = points // 2
    dma = pltpu.SemaphoreType.DMA
    vmem = pl.BlockSpec(memory_space=pltpu.VMEM)
    anywhere = pl.BlockSpec(memory_space=pl.ANY)
    raw, sums = pl.pallas_call(
        kernel,
        out_shape=(
            pltpu.VMEM((K, 2 * N, share), jnp.float32),
            pltpu.VMEM((K, HALF + N, 128), jnp.float32),
        ),
        in_specs=[anywhere] * 3,
        out_specs=[vmem] * 2,
        scratch_shapes=[
            pltpu.VMEM((BINS, 2, M, points), jnp.bfloat16),
            pltpu.VMEM((1, points), jnp.float32),
            pltpu.VMEM((BINS, 2, N, M), jnp.float32),
            pltpu.VMEM((BINS, 4 * N, 2 * M), jnp.bfloat16),
            pltpu.VMEM((BINS, 2, 2 * N, share), jnp.float32),
            pltpu.VMEM((BINS, 2 * M, 2 * M), jnp.float32),
            pltpu.VMEM((BINS, N, 128), jnp.float32),
            pltpu.VMEM((BINS, PLANE, ROWS, 128), jnp.bfloat16),
            pltpu.VMEM((BINS, NZ, ROWS, 128), jnp.bfloat16),
            pltpu.VMEM((PLANE, ROWS, 128), jnp.bfloat16),
            pltpu.SemaphoreType.REGULAR,
            pltpu.SemaphoreType.REGULAR,
            dma((BINS, PARTS)),
            dma((2,)),
            dma((BINS, PARTS)),
            dma((BINS, PARTS)),
            dma((BINS, 2)),
            dma((BINS, 2)),
            dma((2,)),
            dma((BINS,)),
            dma((BINS + 1,)),
            dma((BINS + 1,)),
        ],
        compiler_params=pltpu.CompilerParams(
            collective_id=0, has_side_effects=True, vmem_limit_bytes=32 * 1024 * 1024
        ),
    )(
        pltpu.with_memory_space_constraint(spectra, pltpu.HBM),
        pltpu.with_memory_space_constraint(weights.reshape(1, points), pltpu.HBM),
        pltpu.with_memory_space_constraint(jnp.swapaxes(vectors, 2, 3), pltpu.HBM),
    )
    gram, modes = pl.pallas_call(
        finish_kernel,
        out_shape=(
            jax.ShapeDtypeStruct((K, 2, M, M), jnp.float32),
            jax.ShapeDtypeStruct((K, 2 * N, share), jnp.bfloat16),
        ),
        in_specs=[vmem] * 2,
        out_specs=[anywhere] * 2,
        scratch_shapes=[
            pltpu.VMEM((K, 2, M, M), jnp.float32),
            pltpu.VMEM((K, 2 * N, share), jnp.bfloat16),
            dma((2 * K,)),
        ],
    )(
        pltpu.with_memory_space_constraint(raw, pltpu.VMEM),
        pltpu.with_memory_space_constraint(sums, pltpu.VMEM),
    )
    return gram, modes.reshape(K, 2, N, share)


def solution(mesh):
    return jax.shard_map(
        on_device,
        mesh=mesh,
        in_specs=(P(None, None, "blk", "space"), P("space"), P()),
        out_specs=(P(), P(None, None, None, ("space", "blk"))),
        check_vma=False,
    )
```

```python
import jax
import jax.numpy as jnp
from jax import lax
from jax.experimental import pallas as pl
from jax.experimental.pallas import tpu as pltpu
from jax.sharding import PartitionSpec as P

MESH = pl.DeviceIdType.MESH
K, M, N = 4, 64, 8
NX, NY, NZ = 4, 4, 8
PLANE = NX * NY
BINS = K // 2
HALF = M // 2
ROWS = 48
SPLIT = 1
PARTS = 2 * SPLIT
XY, Z = 0, 1


def ring_distance(d, n):
    return min(d, n - d)


STEPS_XY = sorted(
    ((dx, dy) for dx in range(NX) for dy in range(NY) if dx or dy),
    key=lambda d: -ring_distance(d[0], NX) - ring_distance(d[1], NY),
)
STEPS_Z = sorted(range(1, NZ), key=lambda d: -ring_distance(d, NZ))


def positions():
    return [lax.broadcasted_iota(jnp.int32, (M, 128), d) for d in (0, 1)]


def unpack(packed):
    row, lane = positions()
    packed = packed / M
    held = jnp.concatenate([packed, pltpu.roll(packed, M, 1)], axis=0)
    across = jnp.concatenate([held, held], axis=0).T[:M]
    real = jnp.where(row >= lane, held, across)
    imag = jnp.where(row < lane, held, jnp.where(row > lane, -across, 0.0))
    return real[:, :M], imag[:, :M]


def scale(power):
    lam = jnp.sum(power, axis=1, keepdims=True) / M
    factor = lax.rsqrt(lam + 1e-06)
    return jnp.concatenate([factor, factor], axis=0)


def kernel(
    spec, wts, vec, raw, sums, modes_early, gram_early,
    s_all, w, v, mix, raw_both, raw_early, sums_early, total, power, box_xy, box_z, box_other,
    pair, all_in, load_sem, small_sem, swap_send, swap_recv, sum_send, sum_recv, other_sem, keep_sem, out_send, out_recv,
):
    here = lax.axis_index("space")
    core = lax.axis_index("blk")
    x, y, z = here // (NY * NZ), (here // NZ) % NY, here % NZ
    points = s_all.shape[3]
    share = points // 2
    sibling = (here, 1 - core)
    first = core * BINS
    boxes = {XY: box_xy, Z: box_z}
    slots = {XY: x * NY + y, Z: z}

    barrier = pltpu.get_barrier_semaphore()

    @pl.when(core == 1)
    def _():
        pl.semaphore_signal(barrier, inc=1, device_id=(here, 0), device_id_type=MESH)

    @pl.when(core == 0)
    def _():
        pl.semaphore_wait(barrier, 1)
        pl.semaphore_signal(pair, inc=1, device_id=(here, 1), device_id_type=MESH)

    @pl.when(core == 1)
    def _():
        pl.semaphore_wait(pair, 1)

    w_copy = pltpu.make_async_copy(wts, w, small_sem.at[0])
    v_copy = pltpu.make_async_copy(vec.at[pl.ds(first, BINS)], v, small_sem.at[1])
    v_copy.start()
    w_copy.start()
    rows = pl.ds(pl.multiple_of(core * HALF, HALF), HALF)
    span = share // SPLIT

    def columns(half, part):
        return pl.ds(pl.multiple_of(half * share + part * span, span), span)

    def load(k, part):
        cols = columns(lax.rem(1 - core + part // SPLIT, 2), part % SPLIT)
        return pltpu.make_async_copy(
            spec.at[first + k, :, :, cols], s_all.at[k, :, rows, cols], load_sem.at[k, part]
        )

    def swap(k, part):
        cols = columns(lax.rem(core + part // SPLIT, 2), part % SPLIT)
        return pltpu.make_async_remote_copy(
            src_ref=spec.at[BINS - first + k, :, :, cols],
            dst_ref=s_all.at[k, :, rows, cols],
            send_sem=swap_send.at[k, part],
            recv_sem=swap_recv.at[k, part],
            device_id=sibling,
            device_id_type=MESH,
        )

    for k in range(BINS):
        for part in range(PARTS):
            swap(k, part).start()
            load(k, part).start()

    peers = {
        XY: [((((x + dx) % NX) * NY + (y + dy) % NY) * NZ + z, core) for dx, dy in STEPS_XY],
        Z: [((x * NY + y) * NZ + (z + d) % NZ, core) for d in STEPS_Z],
    }

    @pl.when(core == 1)
    def _():
        for t, _ in peers[XY] + peers[Z]:
            pl.semaphore_signal(barrier, inc=1, device_id=(t, 1), device_id_type=MESH)

    v_copy.wait()
    for k in range(BINS):
        re, im = v[k, 0], v[k, 1]
        both = jnp.concatenate(
            [jnp.concatenate([re, -im], axis=1), jnp.concatenate([im, re], axis=1)], axis=0
        )
        high = both.astype(jnp.bfloat16).astype(jnp.float32)
        mix[k] = jnp.concatenate([high, both - high], axis=0).astype(jnp.bfloat16)
    w_copy.wait()

    row, lane = positions()

    def message(packed, power):
        high = power.astype(jnp.bfloat16).astype(jnp.float32)
        return jnp.concatenate([packed, high, power - high], axis=0).astype(jnp.bfloat16)

    def pack(total):
        turned = pltpu.roll(total, M, 1)
        real = total[:M] + turned[M:]
        imag = turned[:M] - total[M:]
        held = jnp.where(row >= lane, real, imag)
        return jnp.where(lane[:HALF] < M, held[:HALF], pltpu.roll(held, M, 1)[HALF:])

    def send(k, axis, what, both=False):
        box = boxes[axis].at[k, slots[axis]]
        box[...] = what

        def other(t):
            pltpu.make_async_remote_copy(
                src_ref=box,
                dst_ref=box_other.at[slots[axis]],
                send_sem=other_sem.at[0],
                recv_sem=other_sem.at[1],
                device_id=(t, 1 - core),
                device_id_type=MESH,
            ).start()

        for t in peers[axis]:
            pltpu.make_async_remote_copy(
                src_ref=box,
                dst_ref=box,
                send_sem=sum_send.at[k, axis],
                recv_sem=sum_recv.at[k, axis],
                device_id=t,
                device_id_type=MESH,
            ).start()
            if both:
                other(t[0])
        if both:
            other(here)

    def all_others(k, axis):
        return boxes[axis].at[k, pl.ds(0, len(peers[axis]))]

    def gather(k, axis):
        ref = all_others(k, axis)
        pltpu.make_async_copy(ref, ref, sum_recv.at[k, axis]).wait()
        return add_up(boxes[axis][k])

    def add_up(got):
        got = jnp.sum(got.astype(jnp.float32), axis=0)
        return got[:HALF], got[HALF : HALF + N] + got[HALF + N :]

    def to_sibling(i, ours, target):
        return pltpu.make_async_remote_copy(
            src_ref=ours,
            dst_ref=target,
            send_sem=out_send.at[i],
            recv_sem=out_recv.at[i],
            device_id=sibling,
            device_id_type=MESH,
        )

    def keep(where, packed, power):
        where[...] = jnp.concatenate([packed, power], axis=0)

    def finish_early(at, unscaled):
        modes_early[at] = (unscaled * scale(sums_early[at, HALF:])).astype(jnp.bfloat16)
        gram_early[at, 0], gram_early[at, 1] = unpack(sums_early[at, :HALF])

    total[...] = jnp.zeros_like(total)
    power[...] = jnp.zeros_like(power)

    @pl.loop(0, BINS * PARTS)
    def _(i):
        k, part = i // PARTS, i % PARTS
        cols = columns(lax.rem(1 - core + part // SPLIT, 2), part % SPLIT)
        load(k, part).wait()
        swap(k, part).wait_recv()
        s = s_all[k, :, :, cols].reshape(2 * M, span)
        wt = w[:, cols]
        weighted = (s.astype(jnp.float32) * wt).astype(jnp.bfloat16)
        total[k] += lax.dot_general(
            weighted, s, (((1,), (1,)), ((), ())), preferred_element_type=jnp.float32
        )
        r = jnp.dot(mix[k], s, preferred_element_type=jnp.float32)
        raw_both[k, part // SPLIT, :, pl.ds(pl.multiple_of(part % SPLIT * span, span), span)] = r[: 2 * N]
        full = r[: 2 * N] + r[2 * N :]
        square = full * full
        square = (square[:N] + square[N:]) * wt
        power[k] += sum(square[:, g : g + 128] for g in range(0, span, 128))

        @pl.when(i == PARTS - 1)
        def _():
            @pl.when(core == 1)
            def _():
                pl.semaphore_wait(barrier, len(STEPS_XY) + len(STEPS_Z))
                pl.semaphore_signal(all_in, inc=1, device_id=(here, 0), device_id_type=MESH)

            @pl.when(core == 0)
            def _():
                pl.semaphore_wait(all_in, 1)

            send(0, XY, message(pack(total[0]), power[0]))

    send(1, Z, message(pack(total[1]), power[1]))
    own_raw = pltpu.make_async_copy(raw_both.at[1, 1], raw.at[core], keep_sem)
    early_raw = to_sibling(0, raw_both.at[0, 0], raw_early)
    late_raw = to_sibling(1, raw_both.at[1, 0], raw.at[core])
    for copy in (early_raw, late_raw, own_raw):
        copy.start()
    send(0, Z, message(*gather(0, XY)))
    send(1, XY, message(*gather(1, Z)), both=True)
    keep(sums_early.at[core], *gather(0, Z))
    early_sums = to_sibling(2, sums_early.at[core], sums_early.at[core])
    early_sums.start()
    finish_early(core, raw_both[0, 1])
    early_sums.wait()
    early_raw.wait()
    finish_early(1 - core, raw_early[...])
    keep(sums.at[core], *gather(1, XY))
    pltpu.make_async_copy(box_other, box_other, other_sem.at[1]).wait()
    keep(sums.at[1 - core], *add_up(box_other[...]))

    for k in range(BINS):
        for part in range(PARTS):
            swap(k, part).wait_send()
        for axis in (XY, Z):
            ref = all_others(k, axis)
            pltpu.make_async_copy(ref, ref, sum_send.at[k, axis]).wait()
    pltpu.make_async_copy(box_other, box_other, other_sem.at[0]).wait()
    late_raw.wait()
    own_raw.wait()


def finish_kernel(raw, sums, modes_early, gram_early, gram, modes, gram_out, modes_out, sem):
    copies = []

    def write(source, target):
        copies.append(pltpu.make_async_copy(source, target, sem.at[len(copies)]))
        copies[-1].start()

    for c in range(2):
        write(modes_early.at[c], modes.at[BINS * c])
        write(gram_early.at[c], gram.at[BINS * c])
    for c in range(2):
        modes_out[c] = (raw[c] * scale(sums[c, HALF:])).astype(jnp.bfloat16)
        write(modes_out.at[c], modes.at[BINS * c + 1])
    for c in range(2):
        gram_out[c, 0], gram_out[c, 1] = unpack(sums[c, :HALF])
        write(gram_out.at[c], gram.at[BINS * c + 1])
    for copy in copies:
        copy.wait()


def on_device(spectra, weights, vectors):
    points = spectra.shape[3]
    share = points // 2
    dma = pltpu.SemaphoreType.DMA
    vmem = pl.BlockSpec(memory_space=pltpu.VMEM)
    anywhere = pl.BlockSpec(memory_space=pl.ANY)
    early = pl.pallas_call(
        kernel,
        out_shape=(
            pltpu.VMEM((2, 2 * N, share), jnp.float32),
            pltpu.VMEM((2, HALF + N, 128), jnp.float32),
            pltpu.VMEM((2, 2 * N, share), jnp.bfloat16),
            pltpu.VMEM((2, 2, M, M), jnp.float32),
        ),
        in_specs=[anywhere] * 3,
        out_specs=[vmem] * 4,
        scratch_shapes=[
            pltpu.VMEM((BINS, 2, M, points), jnp.bfloat16),
            pltpu.VMEM((1, points), jnp.float32),
            pltpu.VMEM((BINS, 2, N, M), jnp.float32),
            pltpu.VMEM((BINS, 4 * N, 2 * M), jnp.bfloat16),
            pltpu.VMEM((BINS, 2, 2 * N, share), jnp.float32),
            pltpu.VMEM((2 * N, share), jnp.float32),
            pltpu.VMEM((2, HALF + N, 128), jnp.float32),
            pltpu.VMEM((BINS, 2 * M, 2 * M), jnp.float32),
            pltpu.VMEM((BINS, N, 128), jnp.float32),
            pltpu.VMEM((BINS, PLANE, ROWS, 128), jnp.bfloat16),
            pltpu.VMEM((BINS, NZ, ROWS, 128), jnp.bfloat16),
            pltpu.VMEM((PLANE, ROWS, 128), jnp.bfloat16),
            pltpu.SemaphoreType.REGULAR,
            pltpu.SemaphoreType.REGULAR,
            dma((BINS, PARTS)),
            dma((2,)),
            dma((BINS, PARTS)),
            dma((BINS, PARTS)),
            dma((BINS, 2)),
            dma((BINS, 2)),
            dma((2,)),
            dma,
            dma((3,)),
            dma((3,)),
        ],
        compiler_params=pltpu.CompilerParams(
            collective_id=0, has_side_effects=True, vmem_limit_bytes=32 * 1024 * 1024
        ),
    )(
        pltpu.with_memory_space_constraint(spectra, pltpu.HBM),
        pltpu.with_memory_space_constraint(weights.reshape(1, points), pltpu.HBM),
        pltpu.with_memory_space_constraint(jnp.swapaxes(vectors, 2, 3), pltpu.HBM),
    )
    gram, modes = pl.pallas_call(
        finish_kernel,
        out_shape=(
            jax.ShapeDtypeStruct((K, 2, M, M), jnp.float32),
            jax.ShapeDtypeStruct((K, 2 * N, share), jnp.bfloat16),
        ),
        in_specs=[vmem] * 4,
        out_specs=[anywhere] * 2,
        scratch_shapes=[
            pltpu.VMEM((2, 2, M, M), jnp.float32),
            pltpu.VMEM((2, 2 * N, share), jnp.bfloat16),
            dma((2 * K,)),
        ],
    )(*(pltpu.with_memory_space_constraint(a, pltpu.VMEM) for a in early))
    return gram, modes.reshape(K, 2, N, share)


def solution(mesh):
    return jax.shard_map(
        on_device,
        mesh=mesh,
        in_specs=(P(None, None, "blk", "space"), P("space"), P()),
        out_specs=(P(), P(None, None, None, ("space", "blk"))),
        check_vma=False,
    )
```

```python
import jax
import jax.numpy as jnp
from jax import lax
from jax.experimental import pallas as pl
from jax.experimental.pallas import tpu as pltpu
from jax.sharding import PartitionSpec as P

MESH = pl.DeviceIdType.MESH
K, M, N = 4, 64, 8
NX, NY, NZ = 4, 4, 8
PLANE = NX * NY
BINS = K // 2
HALF = M // 2
ROWS = 48
SPLIT = 1
PARTS = 2 * SPLIT
XY, Z = 0, 1


def ring_distance(d, n):
    return min(d, n - d)


STEPS_XY = sorted(
    ((dx, dy) for dx in range(NX) for dy in range(NY) if dx or dy),
    key=lambda d: -ring_distance(d[0], NX) - ring_distance(d[1], NY),
)
STEPS_Z = sorted(range(1, NZ), key=lambda d: -ring_distance(d, NZ))


def positions():
    return [lax.broadcasted_iota(jnp.int32, (M, 128), d) for d in (0, 1)]


def unpack(packed):
    row, lane = positions()
    packed = packed / M
    held = jnp.concatenate([packed, pltpu.roll(packed, M, 1)], axis=0)
    across = jnp.concatenate([held, held], axis=0).T[:M]
    real = jnp.where(row >= lane, held, across)
    imag = jnp.where(row < lane, held, jnp.where(row > lane, -across, 0.0))
    return real[:, :M], imag[:, :M]


def scale(power):
    lam = jnp.sum(power, axis=1, keepdims=True) / M
    factor = lax.rsqrt(lam + 1e-06)
    return jnp.concatenate([factor, factor], axis=0)


def kernel(
    spec, wts, vec, raw, sums, modes_early, gram_early,
    s_all, w, v, mix, raw_both, raw_early, sums_early, total, power, box_xy, box_z, box_other,
    pair, all_in, load_sem, small_sem, swap_send, swap_recv, sum_send, sum_recv, other_sem, keep_sem, out_send, out_recv,
):
    here = lax.axis_index("space")
    core = lax.axis_index("blk")
    x, y, z = here // (NY * NZ), (here // NZ) % NY, here % NZ
    points = s_all.shape[3]
    share = points // 2
    sibling = (here, 1 - core)
    first = core * BINS
    boxes = {XY: box_xy, Z: box_z}
    slots = {XY: x * NY + y, Z: z}

    barrier = pltpu.get_barrier_semaphore()

    @pl.when(core == 1)
    def _():
        pl.semaphore_signal(barrier, inc=1, device_id=(here, 0), device_id_type=MESH)

    @pl.when(core == 0)
    def _():
        pl.semaphore_wait(barrier, 1)
        pl.semaphore_signal(pair, inc=1, device_id=(here, 1), device_id_type=MESH)

    @pl.when(core == 1)
    def _():
        pl.semaphore_wait(pair, 1)

    w_copy = pltpu.make_async_copy(wts, w, small_sem.at[0])
    v_copy = pltpu.make_async_copy(vec.at[pl.ds(first, BINS)], v, small_sem.at[1])
    v_copy.start()
    w_copy.start()
    rows = pl.ds(pl.multiple_of(core * HALF, HALF), HALF)
    span = share // SPLIT

    def columns(half, part):
        return pl.ds(pl.multiple_of(half * share + part * span, span), span)

    def load(k, part):
        cols = columns(lax.rem(1 - core + part // SPLIT, 2), part % SPLIT)
        return pltpu.make_async_copy(
            spec.at[first + k, :, :, cols], s_all.at[k, :, rows, cols], load_sem.at[k, part]
        )

    def swap(k, part):
        cols = columns(lax.rem(core + part // SPLIT, 2), part % SPLIT)
        return pltpu.make_async_remote_copy(
            src_ref=spec.at[BINS - first + k, :, :, cols],
            dst_ref=s_all.at[k, :, rows, cols],
            send_sem=swap_send.at[k, part],
            recv_sem=swap_recv.at[k, part],
            device_id=sibling,
            device_id_type=MESH,
        )

    for k in range(BINS):
        for part in range(PARTS):
            swap(k, part).start()
            load(k, part).start()

    peers = {
        XY: [((((x + dx) % NX) * NY + (y + dy) % NY) * NZ + z, core) for dx, dy in STEPS_XY],
        Z: [((x * NY + y) * NZ + (z + d) % NZ, core) for d in STEPS_Z],
    }

    @pl.when(core == 1)
    def _():
        for t, _ in peers[XY] + peers[Z]:
            pl.semaphore_signal(barrier, inc=1, device_id=(t, 1), device_id_type=MESH)

    v_copy.wait()
    for k in range(BINS):
        re, im = v[k, 0], v[k, 1]
        both = jnp.concatenate(
            [jnp.concatenate([re, -im], axis=1), jnp.concatenate([im, re], axis=1)], axis=0
        )
        high = both.astype(jnp.bfloat16).astype(jnp.float32)
        mix[k] = jnp.concatenate([high, both - high], axis=0).astype(jnp.bfloat16)
    w_copy.wait()

    row, lane = positions()

    def message(packed, power):
        high = power.astype(jnp.bfloat16).astype(jnp.float32)
        return jnp.concatenate([packed, high, power - high], axis=0).astype(jnp.bfloat16)

    def pack(total):
        turned = pltpu.roll(total, M, 1)
        real = total[:M] + turned[M:]
        imag = turned[:M] - total[M:]
        held = jnp.where(row >= lane, real, imag)
        return jnp.where(lane[:HALF] < M, held[:HALF], pltpu.roll(held, M, 1)[HALF:])

    def send(k, axis, what, both=False):
        box = boxes[axis].at[k, slots[axis]]
        box[...] = what

        def other(t):
            pltpu.make_async_remote_copy(
                src_ref=box,
                dst_ref=box_other.at[slots[axis]],
                send_sem=other_sem.at[0],
                recv_sem=other_sem.at[1],
                device_id=(t, 1 - core),
                device_id_type=MESH,
            ).start()

        if both:
            for t, _ in peers[axis]:
                other(t)
        for t in peers[axis]:
            pltpu.make_async_remote_copy(
                src_ref=box,
                dst_ref=box,
                send_sem=sum_send.at[k, axis],
                recv_sem=sum_recv.at[k, axis],
                device_id=t,
                device_id_type=MESH,
            ).start()
        if both:
            other(here)

    def all_others(k, axis):
        return boxes[axis].at[k, pl.ds(0, len(peers[axis]))]

    def gather(k, axis):
        ref = all_others(k, axis)
        pltpu.make_async_copy(ref, ref, sum_recv.at[k, axis]).wait()
        return add_up(boxes[axis][k])

    def add_up(got):
        got = jnp.sum(got.astype(jnp.float32), axis=0)
        return got[:HALF], got[HALF : HALF + N] + got[HALF + N :]

    def to_sibling(i, ours, target):
        return pltpu.make_async_remote_copy(
            src_ref=ours,
            dst_ref=target,
            send_sem=out_send.at[i],
            recv_sem=out_recv.at[i],
            device_id=sibling,
            device_id_type=MESH,
        )

    def keep(where, packed, power):
        where[...] = jnp.concatenate([packed, power], axis=0)

    def finish_early(at, unscaled):
        modes_early[at] = (unscaled * scale(sums_early[at, HALF:])).astype(jnp.bfloat16)
        gram_early[at, 0], gram_early[at, 1] = unpack(sums_early[at, :HALF])

    total[...] = jnp.zeros_like(total)
    power[...] = jnp.zeros_like(power)

    @pl.loop(0, BINS * PARTS)
    def _(i):
        k, part = i // PARTS, i % PARTS
        cols = columns(lax.rem(1 - core + part // SPLIT, 2), part % SPLIT)
        load(k, part).wait()
        swap(k, part).wait_recv()
        s = s_all[k, :, :, cols].reshape(2 * M, span)
        wt = w[:, cols]
        weighted = (s.astype(jnp.float32) * wt).astype(jnp.bfloat16)
        total[k] += lax.dot_general(
            weighted, s, (((1,), (1,)), ((), ())), preferred_element_type=jnp.float32
        )
        r = jnp.dot(mix[k], s, preferred_element_type=jnp.float32)
        raw_both[k, part // SPLIT, :, pl.ds(pl.multiple_of(part % SPLIT * span, span), span)] = r[: 2 * N]
        full = r[: 2 * N] + r[2 * N :]
        square = full * full
        square = (square[:N] + square[N:]) * wt
        power[k] += sum(square[:, g : g + 128] for g in range(0, span, 128))

        @pl.when(i == PARTS - 1)
        def _():
            @pl.when(core == 1)
            def _():
                pl.semaphore_wait(barrier, len(STEPS_XY) + len(STEPS_Z))
                pl.semaphore_signal(all_in, inc=1, device_id=(here, 0), device_id_type=MESH)

            @pl.when(core == 0)
            def _():
                pl.semaphore_wait(all_in, 1)

            send(0, XY, message(pack(total[0]), power[0]))

    send(1, Z, message(pack(total[1]), power[1]))
    own_raw = pltpu.make_async_copy(raw_both.at[1, 1], raw.at[core], keep_sem)
    early_raw = to_sibling(0, raw_both.at[0, 0], raw_early)
    late_raw = to_sibling(1, raw_both.at[1, 0], raw.at[core])
    for copy in (early_raw, late_raw, own_raw):
        copy.start()
    send(0, Z, message(*gather(0, XY)))
    send(1, XY, message(*gather(1, Z)), both=True)
    keep(sums_early.at[core], *gather(0, Z))
    early_sums = to_sibling(2, sums_early.at[core], sums_early.at[core])
    early_sums.start()
    finish_early(core, raw_both[0, 1])
    early_sums.wait()
    early_raw.wait()
    finish_early(1 - core, raw_early[...])
    keep(sums.at[core], *gather(1, XY))
    pltpu.make_async_copy(box_other, box_other, other_sem.at[1]).wait()
    keep(sums.at[1 - core], *add_up(box_other[...]))

    for k in range(BINS):
        for part in range(PARTS):
            swap(k, part).wait_send()
        for axis in (XY, Z):
            ref = all_others(k, axis)
            pltpu.make_async_copy(ref, ref, sum_send.at[k, axis]).wait()
    pltpu.make_async_copy(box_other, box_other, other_sem.at[0]).wait()
    late_raw.wait()
    own_raw.wait()


def finish_kernel(raw, sums, modes_early, gram_early, gram, modes, gram_out, modes_out, sem):
    copies = []

    def write(source, target):
        copies.append(pltpu.make_async_copy(source, target, sem.at[len(copies)]))
        copies[-1].start()

    for c in range(2):
        write(modes_early.at[c], modes.at[BINS * c])
        write(gram_early.at[c], gram.at[BINS * c])
    for c in range(2):
        modes_out[c] = (raw[c] * scale(sums[c, HALF:])).astype(jnp.bfloat16)
        write(modes_out.at[c], modes.at[BINS * c + 1])
    for c in range(2):
        gram_out[c, 0], gram_out[c, 1] = unpack(sums[c, :HALF])
        write(gram_out.at[c], gram.at[BINS * c + 1])
    for copy in copies:
        copy.wait()


def on_device(spectra, weights, vectors):
    points = spectra.shape[3]
    share = points // 2
    dma = pltpu.SemaphoreType.DMA
    vmem = pl.BlockSpec(memory_space=pltpu.VMEM)
    anywhere = pl.BlockSpec(memory_space=pl.ANY)
    early = pl.pallas_call(
        kernel,
        out_shape=(
            pltpu.VMEM((2, 2 * N, share), jnp.float32),
            pltpu.VMEM((2, HALF + N, 128), jnp.float32),
            pltpu.VMEM((2, 2 * N, share), jnp.bfloat16),
            pltpu.VMEM((2, 2, M, M), jnp.float32),
        ),
        in_specs=[anywhere] * 3,
        out_specs=[vmem] * 4,
        scratch_shapes=[
            pltpu.VMEM((BINS, 2, M, points), jnp.bfloat16),
            pltpu.VMEM((1, points), jnp.float32),
            pltpu.VMEM((BINS, 2, N, M), jnp.float32),
            pltpu.VMEM((BINS, 4 * N, 2 * M), jnp.bfloat16),
            pltpu.VMEM((BINS, 2, 2 * N, share), jnp.float32),
            pltpu.VMEM((2 * N, share), jnp.float32),
            pltpu.VMEM((2, HALF + N, 128), jnp.float32),
            pltpu.VMEM((BINS, 2 * M, 2 * M), jnp.float32),
            pltpu.VMEM((BINS, N, 128), jnp.float32),
            pltpu.VMEM((BINS, PLANE, ROWS, 128), jnp.bfloat16),
            pltpu.VMEM((BINS, NZ, ROWS, 128), jnp.bfloat16),
            pltpu.VMEM((PLANE, ROWS, 128), jnp.bfloat16),
            pltpu.SemaphoreType.REGULAR,
            pltpu.SemaphoreType.REGULAR,
            dma((BINS, PARTS)),
            dma((2,)),
            dma((BINS, PARTS)),
            dma((BINS, PARTS)),
            dma((BINS, 2)),
            dma((BINS, 2)),
            dma((2,)),
            dma,
            dma((3,)),
            dma((3,)),
        ],
        compiler_params=pltpu.CompilerParams(
            collective_id=0, has_side_effects=True, vmem_limit_bytes=32 * 1024 * 1024
        ),
    )(
        pltpu.with_memory_space_constraint(spectra, pltpu.HBM),
        pltpu.with_memory_space_constraint(weights.reshape(1, points), pltpu.HBM),
        pltpu.with_memory_space_constraint(jnp.swapaxes(vectors, 2, 3), pltpu.HBM),
    )
    gram, modes = pl.pallas_call(
        finish_kernel,
        out_shape=(
            jax.ShapeDtypeStruct((K, 2, M, M), jnp.float32),
            jax.ShapeDtypeStruct((K, 2 * N, share), jnp.bfloat16),
        ),
        in_specs=[vmem] * 4,
        out_specs=[anywhere] * 2,
        scratch_shapes=[
            pltpu.VMEM((2, 2, M, M), jnp.float32),
            pltpu.VMEM((2, 2 * N, share), jnp.bfloat16),
            dma((2 * K,)),
        ],
    )(*(pltpu.with_memory_space_constraint(a, pltpu.VMEM) for a in early))
    return gram, modes.reshape(K, 2, N, share)


def solution(mesh):
    return jax.shard_map(
        on_device,
        mesh=mesh,
        in_specs=(P(None, None, "blk", "space"), P("space"), P()),
        out_specs=(P(), P(None, None, None, ("space", "blk"))),
        check_vma=False,
    )
```

```python
import jax
import jax.numpy as jnp
from jax import lax
from jax.experimental import pallas as pl
from jax.experimental.pallas import tpu as pltpu
from jax.sharding import PartitionSpec as P

MESH = pl.DeviceIdType.MESH
K, M, N = 4, 64, 8
NX, NY, NZ = 4, 4, 8
PLANE = NX * NY
BINS = K // 2
HALF = M // 2
ROWS = 48
SPLIT = 1
PARTS = 2 * SPLIT
XY, Z = 0, 1


def ring_distance(d, n):
    return min(d, n - d)


STEPS_XY = sorted(
    ((dx, dy) for dx in range(NX) for dy in range(NY) if dx or dy),
    key=lambda d: -ring_distance(d[0], NX) - ring_distance(d[1], NY),
)
STEPS_Z = sorted(range(1, NZ), key=lambda d: -ring_distance(d, NZ))


def positions():
    return [lax.broadcasted_iota(jnp.int32, (M, 128), d) for d in (0, 1)]


def unpack(packed):
    row, lane = positions()
    packed = packed / M
    held = jnp.concatenate([packed, pltpu.roll(packed, M, 1)], axis=0)
    across = jnp.concatenate([held, held], axis=0).T[:M]
    real = jnp.where(row >= lane, held, across)
    imag = jnp.where(row < lane, held, jnp.where(row > lane, -across, 0.0))
    return real[:, :M], imag[:, :M]


def scale(power):
    lam = jnp.sum(power, axis=1, keepdims=True) / M
    factor = lax.rsqrt(lam + 1e-06)
    return jnp.concatenate([factor, factor], axis=0)


def kernel(
    spec, wts, vec, raw, sums, modes_early, gram_early,
    s_all, w, v, mix, raw_both, raw_early, sums_early, total, power, box_xy, box_z, box_other,
    pair, all_in, load_sem, small_sem, swap_send, swap_recv, sum_send, sum_recv, other_sem, keep_sem, out_send, out_recv,
):
    here = lax.axis_index("space")
    core = lax.axis_index("blk")
    x, y, z = here // (NY * NZ), (here // NZ) % NY, here % NZ
    points = s_all.shape[3]
    share = points // 2
    sibling = (here, 1 - core)
    first = core * BINS
    boxes = {XY: box_xy, Z: box_z}
    slots = {XY: x * NY + y, Z: z}

    barrier = pltpu.get_barrier_semaphore()

    @pl.when(core == 1)
    def _():
        pl.semaphore_signal(barrier, inc=1, device_id=(here, 0), device_id_type=MESH)

    @pl.when(core == 0)
    def _():
        pl.semaphore_wait(barrier, 1)
        pl.semaphore_signal(pair, inc=1, device_id=(here, 1), device_id_type=MESH)

    @pl.when(core == 1)
    def _():
        pl.semaphore_wait(pair, 1)

    w_copy = pltpu.make_async_copy(wts, w, small_sem.at[0])
    v_copy = pltpu.make_async_copy(vec.at[pl.ds(first, BINS)], v, small_sem.at[1])
    v_copy.start()
    w_copy.start()
    rows = pl.ds(pl.multiple_of(core * HALF, HALF), HALF)
    span = share // SPLIT

    def columns(half, part):
        return pl.ds(pl.multiple_of(half * share + part * span, span), span)

    def load(k, part):
        cols = columns(lax.rem(1 - core + part // SPLIT, 2), part % SPLIT)
        return pltpu.make_async_copy(
            spec.at[first + k, :, :, cols], s_all.at[k, :, rows, cols], load_sem.at[k, part]
        )

    def swap(k, part):
        cols = columns(lax.rem(core + part // SPLIT, 2), part % SPLIT)
        return pltpu.make_async_remote_copy(
            src_ref=spec.at[BINS - first + k, :, :, cols],
            dst_ref=s_all.at[k, :, rows, cols],
            send_sem=swap_send.at[k, part],
            recv_sem=swap_recv.at[k, part],
            device_id=sibling,
            device_id_type=MESH,
        )

    for k in range(BINS):
        for part in range(PARTS):
            swap(k, part).start()
            load(k, part).start()

    peers = {
        XY: [((((x + dx) % NX) * NY + (y + dy) % NY) * NZ + z, core) for dx, dy in STEPS_XY],
        Z: [((x * NY + y) * NZ + (z + d) % NZ, core) for d in STEPS_Z],
    }

    @pl.when(core == 1)
    def _():
        for t, _ in peers[XY] + peers[Z]:
            pl.semaphore_signal(barrier, inc=1, device_id=(t, 1), device_id_type=MESH)

    v_copy.wait()
    for k in range(BINS):
        re, im = v[k, 0], v[k, 1]
        both = jnp.concatenate(
            [jnp.concatenate([re, -im], axis=1), jnp.concatenate([im, re], axis=1)], axis=0
        )
        high = both.astype(jnp.bfloat16).astype(jnp.float32)
        mix[k] = jnp.concatenate([high, both - high], axis=0).astype(jnp.bfloat16)
    w_copy.wait()

    row, lane = positions()

    def message(packed, power):
        high = power.astype(jnp.bfloat16).astype(jnp.float32)
        return jnp.concatenate([packed, high, power - high], axis=0).astype(jnp.bfloat16)

    def pack(total):
        turned = pltpu.roll(total, M, 1)
        real = total[:M] + turned[M:]
        imag = turned[:M] - total[M:]
        held = jnp.where(row >= lane, real, imag)
        return jnp.where(lane[:HALF] < M, held[:HALF], pltpu.roll(held, M, 1)[HALF:])

    def send(k, axis, what, both=False):
        box = boxes[axis].at[k, slots[axis]]
        box[...] = what

        def other(t):
            pltpu.make_async_remote_copy(
                src_ref=box,
                dst_ref=box_other.at[slots[axis]],
                send_sem=other_sem.at[0],
                recv_sem=other_sem.at[1],
                device_id=(t, 1 - core),
                device_id_type=MESH,
            ).start()

        if both:
            for t, _ in peers[axis]:
                other(t)
        for t in peers[axis]:
            pltpu.make_async_remote_copy(
                src_ref=box,
                dst_ref=box,
                send_sem=sum_send.at[k, axis],
                recv_sem=sum_recv.at[k, axis],
                device_id=t,
                device_id_type=MESH,
            ).start()
        if both:
            other(here)

    def all_others(k, axis):
        return boxes[axis].at[k, pl.ds(0, len(peers[axis]))]

    def gather(k, axis):
        ref = all_others(k, axis)
        pltpu.make_async_copy(ref, ref, sum_recv.at[k, axis]).wait()
        return add_up(boxes[axis][k])

    def add_up(got):
        got = jnp.sum(got.astype(jnp.float32), axis=0)
        return got[:HALF], got[HALF : HALF + N] + got[HALF + N :]

    def to_sibling(i, ours, target):
        return pltpu.make_async_remote_copy(
            src_ref=ours,
            dst_ref=target,
            send_sem=out_send.at[i],
            recv_sem=out_recv.at[i],
            device_id=sibling,
            device_id_type=MESH,
        )

    def keep(where, packed, power):
        where[...] = jnp.concatenate([packed, power], axis=0)

    def finish_early(at, unscaled):
        modes_early[at] = (unscaled * scale(sums_early[at, HALF:])).astype(jnp.bfloat16)
        gram_early[at, 0], gram_early[at, 1] = unpack(sums_early[at, :HALF])

    total[...] = jnp.zeros_like(total)
    power[...] = jnp.zeros_like(power)

    @pl.loop(0, BINS * PARTS)
    def _(i):
        k, part = i // PARTS, i % PARTS
        cols = columns(lax.rem(1 - core + part // SPLIT, 2), part % SPLIT)
        load(k, part).wait()
        swap(k, part).wait_recv()
        s = s_all[k, :, :, cols].reshape(2 * M, span)
        wt = w[:, cols]
        weighted = (s.astype(jnp.float32) * wt).astype(jnp.bfloat16)
        total[k] += lax.dot_general(
            weighted, s, (((1,), (1,)), ((), ())), preferred_element_type=jnp.float32
        )
        r = jnp.dot(mix[k], s, preferred_element_type=jnp.float32)
        raw_both[k, part // SPLIT, :, pl.ds(pl.multiple_of(part % SPLIT * span, span), span)] = r[: 2 * N]
        full = r[: 2 * N] + r[2 * N :]
        square = full * full
        square = (square[:N] + square[N:]) * wt
        power[k] += sum(square[:, g : g + 128] for g in range(0, span, 128))

        @pl.when(i == PARTS - 1)
        def _():
            @pl.when(core == 1)
            def _():
                pl.semaphore_wait(barrier, len(STEPS_XY) + len(STEPS_Z))
                pl.semaphore_signal(all_in, inc=1, device_id=(here, 0), device_id_type=MESH)

            @pl.when(core == 0)
            def _():
                pl.semaphore_wait(all_in, 1)

            send(0, XY, message(pack(total[0]), power[0]))

    send(1, Z, message(pack(total[1]), power[1]))
    own_raw = pltpu.make_async_copy(raw_both.at[1, 1], raw.at[core], keep_sem)
    early_raw = to_sibling(0, raw_both.at[0, 0], raw_early)
    late_raw = to_sibling(1, raw_both.at[1, 0], raw.at[core])
    send(0, Z, message(*gather(0, XY)))
    send(1, XY, message(*gather(1, Z)), both=True)
    for copy in (early_raw, late_raw, own_raw):
        copy.start()
    keep(sums_early.at[core], *gather(0, Z))
    early_sums = to_sibling(2, sums_early.at[core], sums_early.at[core])
    early_sums.start()
    finish_early(core, raw_both[0, 1])
    early_sums.wait()
    early_raw.wait()
    finish_early(1 - core, raw_early[...])
    pltpu.make_async_copy(box_other, box_other, other_sem.at[1]).wait()
    keep(sums.at[1 - core], *add_up(box_other[...]))
    keep(sums.at[core], *gather(1, XY))

    for k in range(BINS):
        for part in range(PARTS):
            swap(k, part).wait_send()
        for axis in (XY, Z):
            ref = all_others(k, axis)
            pltpu.make_async_copy(ref, ref, sum_send.at[k, axis]).wait()
    pltpu.make_async_copy(box_other, box_other, other_sem.at[0]).wait()
    late_raw.wait()
    own_raw.wait()


def finish_kernel(raw, sums, modes_early, gram_early, gram, modes, gram_out, modes_out, sem):
    copies = []

    def write(source, target):
        copies.append(pltpu.make_async_copy(source, target, sem.at[len(copies)]))
        copies[-1].start()

    for c in range(2):
        write(modes_early.at[c], modes.at[BINS * c])
        write(gram_early.at[c], gram.at[BINS * c])
    for c in range(2):
        modes_out[c] = (raw[c] * scale(sums[c, HALF:])).astype(jnp.bfloat16)
        write(modes_out.at[c], modes.at[BINS * c + 1])
    for c in range(2):
        gram_out[c, 0], gram_out[c, 1] = unpack(sums[c, :HALF])
        write(gram_out.at[c], gram.at[BINS * c + 1])
    for copy in copies:
        copy.wait()


def on_device(spectra, weights, vectors):
    points = spectra.shape[3]
    share = points // 2
    dma = pltpu.SemaphoreType.DMA
    vmem = pl.BlockSpec(memory_space=pltpu.VMEM)
    anywhere = pl.BlockSpec(memory_space=pl.ANY)
    early = pl.pallas_call(
        kernel,
        out_shape=(
            pltpu.VMEM((2, 2 * N, share), jnp.float32),
            pltpu.VMEM((2, HALF + N, 128), jnp.float32),
            pltpu.VMEM((2, 2 * N, share), jnp.bfloat16),
            pltpu.VMEM((2, 2, M, M), jnp.float32),
        ),
        in_specs=[anywhere] * 3,
        out_specs=[vmem] * 4,
        scratch_shapes=[
            pltpu.VMEM((BINS, 2, M, points), jnp.bfloat16),
            pltpu.VMEM((1, points), jnp.float32),
            pltpu.VMEM((BINS, 2, N, M), jnp.float32),
            pltpu.VMEM((BINS, 4 * N, 2 * M), jnp.bfloat16),
            pltpu.VMEM((BINS, 2, 2 * N, share), jnp.float32),
            pltpu.VMEM((2 * N, share), jnp.float32),
            pltpu.VMEM((2, HALF + N, 128), jnp.float32),
            pltpu.VMEM((BINS, 2 * M, 2 * M), jnp.float32),
            pltpu.VMEM((BINS, N, 128), jnp.float32),
            pltpu.VMEM((BINS, PLANE, ROWS, 128), jnp.bfloat16),
            pltpu.VMEM((BINS, NZ, ROWS, 128), jnp.bfloat16),
            pltpu.VMEM((PLANE, ROWS, 128), jnp.bfloat16),
            pltpu.SemaphoreType.REGULAR,
            pltpu.SemaphoreType.REGULAR,
            dma((BINS, PARTS)),
            dma((2,)),
            dma((BINS, PARTS)),
            dma((BINS, PARTS)),
            dma((BINS, 2)),
            dma((BINS, 2)),
            dma((2,)),
            dma,
            dma((3,)),
            dma((3,)),
        ],
        compiler_params=pltpu.CompilerParams(
            collective_id=0, has_side_effects=True, vmem_limit_bytes=32 * 1024 * 1024
        ),
    )(
        pltpu.with_memory_space_constraint(spectra, pltpu.HBM),
        pltpu.with_memory_space_constraint(weights.reshape(1, points), pltpu.HBM),
        pltpu.with_memory_space_constraint(jnp.swapaxes(vectors, 2, 3), pltpu.HBM),
    )
    gram, modes = pl.pallas_call(
        finish_kernel,
        out_shape=(
            jax.ShapeDtypeStruct((K, 2, M, M), jnp.float32),
            jax.ShapeDtypeStruct((K, 2 * N, share), jnp.bfloat16),
        ),
        in_specs=[vmem] * 4,
        out_specs=[anywhere] * 2,
        scratch_shapes=[
            pltpu.VMEM((2, 2, M, M), jnp.float32),
            pltpu.VMEM((2, 2 * N, share), jnp.bfloat16),
            dma((2 * K,)),
        ],
    )(*(pltpu.with_memory_space_constraint(a, pltpu.VMEM) for a in early))
    return gram, modes.reshape(K, 2, N, share)


def solution(mesh):
    return jax.shard_map(
        on_device,
        mesh=mesh,
        in_specs=(P(None, None, "blk", "space"), P("space"), P()),
        out_specs=(P(), P(None, None, None, ("space", "blk"))),
        check_vma=False,
    )
```
